256 devices in a mesh: pipe: 8 (over x, y_hi), expert: 32 (over z, y_lo, core).
Axes of the slice: x: 4, y: 4 (y_hi: 2, y_lo: 2; y = y_hi * 2 + y_lo), z: 8, core: 2. Of those that a mesh axis runs over, the one named last changes fastest.
Arguments:
- out_grad: bfloat16 [8, 2, 1024, 2048], P('pipe', None, 'expert'), may hold values from -6 to 6
- moe_input: bfloat16 [8, 2, 1024, 2048], P('pipe', None, 'expert'), may hold values from -6 to 6
- expert_input: bfloat16 [8, 32, 2, 32, 9, 2048], P('pipe', 'expert'), may hold values from -6 to 6
- expert_gate: bfloat16 [8, 32, 2, 32, 9, 768], P('pipe', 'expert'), may hold values from -6 to 6
- expert_ids: int32 [8, 2, 1024, 8], P('pipe', None, 'expert'), may hold values from 0 to 31, all different within a row; in each aligned block of 32 rows (0 to 31, 32 to 63, ..., all dimensions but the last counted through in order) at most 9 rows name the same one
- top_logits: float32 [8, 2, 1024, 8], P('pipe', None, 'expert'), may hold values from -4 to 300
- inv_rms: float32 [8, 2, 1024], P('pipe', None, 'expert'), may hold values from 0.5 to 5
- norm_gain: bfloat16 [8, 2048], P('pipe'), may hold values from 0.5 to 1.5
- w_gate: bfloat16 [8, 32, 2048, 768], P('pipe', 'expert'), may hold values from -0.125 to 0.125
- w_up: bfloat16 [8, 32, 2048, 768], P('pipe', 'expert'), may hold values from -0.125 to 0.125
- w_down: bfloat16 [8, 32, 768, 2048], P('pipe', 'expert'), may hold values from -0.21875 to 0.21875
- router: bfloat16 [8, 2048, 32], P('pipe'), may hold values from -0.125 to 0.125
Outputs:
- upstream_grad: bfloat16 [8, 2, 1024, 2048], P('pipe', None, 'expert')
The draws below stay inside these ranges and needn't reach their ends.
Inputs may be any that keep to these rules, and one draw needn't show every extreme that they name: `expert_ids`: each token names 8 different experts. Among the tokens of one sub-micro-batch on one index of expert (aligned blocks of 32 rows), no expert is named more than 9 times, a bound that some block reaches.
All inputs are finite; a program needn't handle non-finite values.
Results may differ from the reference program's by a relative error of at most 0.0051.
Values may be sent and summed in bfloat16 or wider, within the bound.
No kernel may reach another device: no remote copies, remote signals or barrier semaphores. Data moves between devices by JAX's collectives and lax.ppermute only.
A program may use at most 128 MiB of HBM per device.

```python
import math
from functools import partial
import jax
import jax.numpy as jnp
import numpy as np
from jax import lax

D = 2048
H = 768
TOPK = 8
TOK = 32
EXPERTS = 32
CAP = 9
TOKENS = 1024
N_PIPE = 8
N_EXPERT = 32


def draw_top_logits(key, part):
    key = jax.random.fold_in(key, 11)
    full_shape = (N_PIPE, 2, TOKENS, TOPK)
    row_shape = (N_PIPE, 2, TOKENS, 1)
    key_shift, key_spread = jax.random.split(key, 2)
    row_shift = jax.random.uniform(key_shift, row_shape, jnp.float32, -4.0, 4.0)
    return row_shift + jax.random.uniform(key_spread, full_shape, jnp.float32, 0.0, 2.5)


def block_levels(key, shape, cuts, smallest, largest):
    def one(axis_at, parts):
        heights = jax.random.uniform(jax.random.fold_in(jax.random.fold_in(key, 6), axis_at), (parts,), jnp.float32, smallest / len(cuts), largest / len(cuts))
        return jnp.repeat(jnp.exp(heights), shape[axis_at] // parts).reshape((-1,) + (1,) * (len(shape) - axis_at - 1))

    loudness = one(*cuts[0])
    for cut in cuts[1:]:
        loudness = loudness * one(*cut)
    return loudness


def shared_out(stream_key, own, number, rows, count, top, limit, lean):
    sequence = jax.random.permutation(stream_key, count)
    heavy_load, common = shares(count, rows * top, limit, lean, True), shares(count, rows * top, limit, lean, False)
    places = jnp.arange(count)

    def named(tallies, offset_by):
        used = int((tallies > 0).sum())
        fixed = max(1, used // 4)
        passed = fixed + (places - fixed + offset_by * (used - fixed)) % max(1, count - fixed)
        return jnp.zeros((count,), jnp.int32).at[sequence[jnp.where(places < fixed, places, passed)]].set(jnp.asarray(tallies, jnp.int32))

    tallies = jnp.where(number % 4 == 0, named(heavy_load, number // 4), named(common, number - number // 4 - 1))
    mixed = jax.random.permutation(jax.random.fold_in(own, 3), count)
    source_of, taker = mixed[0:count // 2 * 2:2], mixed[1:count // 2 * 2:2]
    slack = jnp.minimum(tallies[source_of] - 1, limit - tallies[taker]) // 2
    slack = jnp.where((source_of == sequence[0]) | (taker == sequence[0]) | (tallies[taker] == 0), 0, jnp.maximum(slack, 0))
    passed = jax.random.randint(jax.random.fold_in(own, 4), (count // 2,), 0, 1 << 20) % (slack + 1)
    tallies = tallies.at[source_of].add(-passed).at[taker].add(passed)
    members = jnp.searchsorted(jnp.cumsum(tallies), jnp.arange(rows * top), side="right").astype(jnp.int32)
    listing = members.reshape(top, rows).T
    listing = listing[jax.random.permutation(jax.random.fold_in(own, 1), rows)]
    offset_by = jax.random.randint(jax.random.fold_in(own, 2), (rows, 1), 0, top)
    return jnp.take_along_axis(listing, (jnp.arange(top)[None, :] + offset_by) % top, axis=1)


def shares(number_of, total, most, lean, full):
    portions = [(1 << 20) // math.isqrt(rank ** lean) + 1 for rank in range(1, number_of + 1)]
    largest = most if full else min(most, max(-(-total // number_of), total * portions[0] // sum(portions)))
    least = 1 if total - largest >= number_of - 1 else 0
    given, spare = [largest] + [least] * (number_of - 1), total - largest - least * (number_of - 1)
    while spare > 0:
        movable = [i for i in range(1, number_of) if given[i] < largest] or [i for i in range(1, number_of) if given[i] < most]
        mass, budget = sum([portions[i] for i in movable]), spare
        for i in movable:
            addition = min(most - given[i], max(1, budget * portions[i] // mass), spare)
            given[i] = given[i] + addition
            spare = spare - addition
    return np.array(given)


def gaussian(key, extent, deviation, most, cuts=(), kind=jnp.bfloat16):
    factor_of = block_levels(key, extent, cuts, -0.22, 0.18) if cuts else 1.0
    entries = jax.random.normal(key, extent, jnp.float32) * deviation * factor_of
    return jnp.minimum(jnp.maximum(entries, -most), most).astype(kind)


def setup_inputs(seed: int = 0) -> dict:
    seeds = jax.random.split(jax.random.key(seed), 13)
    out_grad = gaussian(seeds[0], (N_PIPE, 2, TOKENS, D), 1.0, 6.0, ((0, 8), (2, 32)))
    moe_input = gaussian(seeds[1], (N_PIPE, 2, TOKENS, D), 1.0, 6.0, ((0, 8), (2, 32)))
    expert_input = gaussian(seeds[2], (N_PIPE, EXPERTS, 2, N_EXPERT, CAP, D), 1.0, 6.0, ((0, 8), (1, 32)))
    expert_gate = gaussian(seeds[3], (N_PIPE, EXPERTS, 2, N_EXPERT, CAP, H), 1.5, 6.0, ((0, 8), (1, 32)))
    expert_ids_keys = jax.random.split(jax.random.fold_in(seeds[4], 1), N_PIPE * 2 * TOKENS // TOK)
    expert_ids_turns = jax.random.permutation(jax.random.fold_in(seeds[4], 3), N_PIPE * 2 * TOKENS // TOK)
    expert_ids = jax.vmap(lambda own, number: shared_out(jax.random.fold_in(seeds[4], 2), own, number, TOK, EXPERTS, TOPK, CAP, 1))(expert_ids_keys, expert_ids_turns).reshape((N_PIPE, 2, TOKENS, TOPK))
    top_logits = draw_top_logits(jax.random.fold_in(seeds[12], 71), 0)
    inv_rms = jnp.clip(jnp.exp(math.log(5.0) - 2.3025851 * jax.random.uniform(seeds[6], (N_PIPE, 2, TOKENS), jnp.float32) ** block_levels(seeds[6], (N_PIPE, 2, TOKENS), ((0, 8), (2, 32)), -0.2, 0.2)), 0.5, 5.0)
    norm_gain = jnp.clip(1.0 + 0.1 * jax.random.normal(seeds[7], (N_PIPE, D), jnp.float32), 0.5, 1.5).astype(jnp.bfloat16)
    w_gate = gaussian(seeds[8], (N_PIPE, EXPERTS, D, H), D ** -0.5, 0.125, ((0, 8), (1, 32)))
    w_up = gaussian(seeds[9], (N_PIPE, EXPERTS, D, H), D ** -0.5, 0.125, ((0, 8), (1, 32)))
    w_down = gaussian(seeds[10], (N_PIPE, EXPERTS, H, D), H ** -0.5, 0.21875, ((0, 8), (1, 32)))
    router = gaussian(seeds[11], (N_PIPE, D, EXPERTS), D ** -0.5, 0.125, ((0, 8),))
    return dict(out_grad=out_grad, moe_input=moe_input, expert_input=expert_input, expert_gate=expert_gate, expert_ids=expert_ids, top_logits=top_logits, inv_rms=inv_rms, norm_gain=norm_gain, w_gate=w_gate, w_up=w_up, w_down=w_down, router=router)


def slot_table(id_rows, experts, capacity):
    flat_ids = id_rows.reshape(-1).astype(jnp.int32)
    row_count = flat_ids.shape[0]
    onehot = (flat_ids[:, None] == jnp.arange(experts, dtype=jnp.int32)[None, :]).astype(jnp.int32)
    rank_table = (jnp.cumsum(onehot, axis=0) - 1).astype(jnp.int32)
    slot_rank = lax.optimization_barrier(jnp.sum(onehot * rank_table, axis=1)).astype(jnp.int32)
    slot_index = (flat_ids * capacity + slot_rank).astype(jnp.int32)
    source = jnp.full((experts * capacity,), row_count, jnp.int32)
    source = source.at[slot_index].set(jnp.arange(row_count, dtype=jnp.int32))
    return (slot_index, source)

def dispatch(grad_rows, source, top_count):
    row_count = grad_rows.shape[0] * top_count
    is_live = source < row_count
    safe_src = jnp.where(is_live, source, 0).astype(jnp.int32)
    token_index = (safe_src // top_count).astype(jnp.int32)
    return jnp.where(is_live[:, None], grad_rows[token_index], jnp.zeros((), grad_rows.dtype))

def expert_rows(input_rows, grad_rows, gate_rows, gate_mat, up_mat, down_mat):
    contract = (((1,), (1,)), ((), ()))
    up_proj = jnp.dot(input_rows, up_mat, preferred_element_type=jnp.float32)
    down_back = lax.dot_general(grad_rows, down_mat, contract, preferred_element_type=jnp.float32)
    gate_pre = gate_rows.astype(jnp.float32)
    sigmoid_gate = jax.nn.sigmoid(gate_pre)
    activated = gate_pre * sigmoid_gate
    weight_grad = lax.optimization_barrier(jnp.sum(down_back * activated * up_proj, axis=-1)).astype(jnp.bfloat16)
    d_gate = (down_back * up_proj * sigmoid_gate * (1.0 + gate_pre * (1.0 - sigmoid_gate))).astype(jnp.bfloat16)
    d_up = (down_back * activated).astype(jnp.bfloat16)
    row_grad = lax.dot_general(d_gate, gate_mat, contract, preferred_element_type=jnp.float32)
    row_grad = row_grad + lax.dot_general(d_up, up_mat, contract, preferred_element_type=jnp.float32)
    return (row_grad.astype(jnp.bfloat16), weight_grad)

def token_grad(grad_rows, input_rows, logit_rows, id_rows, rms_rows, gain_row, router_mat, pair_grad, pair_weight):
    gate_probs = jax.nn.softmax(logit_rows.astype(jnp.float32), axis=-1)
    mixed_grad = lax.optimization_barrier(jnp.sum(gate_probs[:, :, None] * pair_grad.astype(jnp.float32), axis=1))
    weight_f = pair_weight.astype(jnp.float32)
    centred = weight_f - lax.optimization_barrier(jnp.sum(gate_probs * weight_f, axis=-1, keepdims=True))
    logit_grad = gate_probs * centred
    picked = (id_rows[:, :, None] == jnp.arange(router_mat.shape[1], dtype=jnp.int32)[None, None, :]).astype(jnp.float32)
    full_grad = lax.optimization_barrier(jnp.sum(logit_grad[:, :, None] * picked, axis=1))
    routed = jnp.dot(full_grad, router_mat.astype(jnp.float32).T, precision=lax.Precision.HIGHEST)
    input_grad = mixed_grad + routed
    gain_f = gain_row.astype(jnp.float32)
    normed = input_rows.astype(jnp.float32) / gain_f
    scaled = gain_f * input_grad
    inner_mean = lax.optimization_barrier(jnp.mean(scaled * normed, axis=-1, keepdims=True))
    result = grad_rows.astype(jnp.float32) + rms_rows[:, None] * (scaled - normed * inner_mean)
    return result.astype(jnp.bfloat16)

def expert_apply(operands):
    return expert_rows(operands[0], operands[1], operands[2], operands[3], operands[4], operands[5])

def pick_rows(table, index):
    return table[index]

def one_block(out_grad, moe_input, saved_input, saved_gate, expert_ids, top_logits, inv_rms, norm_gain, w_gate, w_up, w_down, router):
    ids_blocks = expert_ids.reshape(N_EXPERT, TOK, TOPK)
    input_blocks = moe_input.reshape(N_EXPERT, TOK, D)
    grad_blocks = out_grad.reshape(N_EXPERT, TOK, D)
    slot_index, source = jax.vmap(partial(slot_table, experts=EXPERTS, capacity=CAP))(ids_blocks)
    sent_grad = jax.vmap(partial(dispatch, top_count=TOPK))(grad_blocks, source)
    arranged = sent_grad.reshape(N_EXPERT, EXPERTS, CAP, D).transpose(1, 0, 2, 3).reshape(EXPERTS, N_EXPERT * CAP, D)
    rows_input = saved_input.reshape(EXPERTS, N_EXPERT * CAP, D)
    rows_gate = saved_gate.reshape(EXPERTS, N_EXPERT * CAP, H)
    grads, weights = lax.map(expert_apply, (rows_input, arranged, rows_gate, w_gate, w_up, w_down))
    grads_back = grads.reshape(EXPERTS, N_EXPERT, CAP, D).transpose(1, 0, 2, 3).reshape(N_EXPERT, EXPERTS * CAP, D)
    weights_back = weights.reshape(EXPERTS, N_EXPERT, CAP).transpose(1, 0, 2).reshape(N_EXPERT, EXPERTS * CAP)
    pair_grad = jax.vmap(pick_rows)(grads_back, slot_index).reshape(N_EXPERT, TOK, TOPK, D)
    pair_weight = jax.vmap(pick_rows)(weights_back, slot_index).reshape(N_EXPERT, TOK, TOPK)
    logit_blocks = top_logits.reshape(N_EXPERT, TOK, TOPK)
    rms_blocks = inv_rms.reshape(N_EXPERT, TOK)
    result = jax.vmap(token_grad, in_axes=(0, 0, 0, 0, 0, None, None, 0, 0))(grad_blocks, input_blocks, logit_blocks, ids_blocks, rms_blocks, norm_gain, router, pair_grad, pair_weight)
    return result.reshape(TOKENS, D)

def reference(out_grad, moe_input, expert_input, expert_gate, expert_ids, top_logits, inv_rms, norm_gain, w_gate, w_up, w_down, router):
    section_grads = []
    for section in range(N_PIPE):
        halves = []
        for sub_batch in range(2):
            halves.append(one_block(out_grad[section, sub_batch], moe_input[section, sub_batch], expert_input[section, :, sub_batch], expert_gate[section, :, sub_batch], expert_ids[section, sub_batch], top_logits[section, sub_batch], inv_rms[section, sub_batch], norm_gain[section], w_gate[section], w_up[section], w_down[section], router[section]))
        section_grads.append(jnp.stack(halves))
    layer_grad = jnp.stack(section_grads)
    from_above = jnp.concatenate([layer_grad[1:, 0], jnp.zeros_like(layer_grad[:1, 0])], axis=0)
    from_below = jnp.concatenate([jnp.zeros_like(layer_grad[:1, 1]), layer_grad[:-1, 1]], axis=0)
    return jnp.stack([from_above, from_below], axis=1)
```

```python
import jax
import jax.numpy as jnp
import numpy as np
from jax import lax
from jax.experimental import pallas as pl
from jax.experimental.pallas import tpu as pltpu
from jax.sharding import PartitionSpec as P

PLANES = 8
GROUPS = 4
TOK = 32
TOPK = 8
CAP = 9
D = 2048
H = 768
EXTRA = 128
W = D + EXTRA
SLOTS = CAP * PLANES
ROWS = GROUPS * SLOTS
COLUMN = PLANES * TOK
NT = (((1,), (1,)), ((), ()))
TN = (((0,), (0,)), ((), ()))
F32 = jnp.float32
BF16 = jnp.bfloat16

SLOT_Q = np.repeat(np.arange(GROUPS), SLOTS).astype(np.int32)
SLOT_R = np.tile(np.repeat(np.arange(CAP), PLANES), GROUPS).astype(np.int32)
SLOT_O = np.tile(np.arange(PLANES), GROUPS * CAP).astype(np.int32)
SLOT_ROW = np.stack([SLOT_Q, SLOT_R, SLOT_O] + [SLOT_O] * 5)
SLOT_COL = np.ascontiguousarray(SLOT_ROW.T)

VMEM = pl.BlockSpec(memory_space=pltpu.VMEM)
SMEM = pl.BlockSpec(memory_space=pltpu.SMEM)
LIMIT = 56 * 1024 * 1024


def call(kernel, outs, n_in, flops=0, nbytes=0, smem_first=True):
    specs = [VMEM] * n_in
    if smem_first:
        specs = [SMEM] + specs
    return pl.pallas_call(
        kernel,
        out_shape=outs,
        in_specs=specs,
        out_specs=jax.tree.map(lambda _: VMEM, outs),
        compiler_params=pltpu.CompilerParams(vmem_limit_bytes=LIMIT),
        cost_estimate=pl.CostEstimate(flops=flops, bytes_accessed=nbytes, transcendentals=0),
    )


def shape(dims, dtype=BF16):
    return jax.ShapeDtypeStruct(dims, dtype)


def dot(a, b, dims=(((1,), (0,)), ((), ()))):
    return lax.dot_general(a, b, dims, preferred_element_type=F32)


def split3(value):
    high = value.astype(BF16)
    rest = value - high.astype(F32)
    middle = rest.astype(BF16)
    low = (rest - middle.astype(F32)).astype(BF16)
    return high, middle, low


def prep_kernel(grad_ref, ids_ref, logit_ref, first_ref, second_ref):
    row = lax.broadcasted_iota(jnp.int32, (TOK, TOK), 0)
    col = lax.broadcasted_iota(jnp.int32, (TOK, TOK), 1)
    eye = jnp.where(row == col, 1.0, 0.0).astype(BF16)
    for b, out_ref in enumerate((first_ref, second_ref)):
        logits = logit_ref[b]
        raised = jnp.exp(logits - jnp.max(logits, axis=0, keepdims=True))
        probs = raised / jnp.sum(raised, axis=0, keepdims=True)
        high, middle, low = split3(probs)
        stack = jnp.concatenate(
            [
                ids_ref[b].astype(F32),
                high.astype(F32),
                middle.astype(F32),
                low.astype(F32),
                jnp.zeros((EXTRA - 4 * TOPK, TOK), F32),
            ],
            axis=0,
        ).astype(BF16)
        out_ref[:, :D] = grad_ref[b]
        out_ref[:, D:] = dot(eye, stack, NT).astype(BF16)


def saved_kernel(place_ref, x_ref, gate_ref, slot_ref, up_mat_ref, up_ref, gate_out_ref):
    plane, group = place_ref[0], place_ref[1]
    q, r, o = slot_ref[:, 0:1], slot_ref[:, 1:2], slot_ref[:, 2:3]
    wanted = r * (PLANES * GROUPS) + ((plane + o) & (PLANES - 1)) * GROUPS + (q ^ group)
    picks = jnp.where(
        wanted == lax.broadcasted_iota(jnp.int32, (ROWS, ROWS), 1), 1.0, 0.0
    ).astype(BF16)
    for b in range(2):
        rows = dot(picks, x_ref[b]).astype(BF16)
        up_ref[b] = dot(rows, up_mat_ref[...])
        gate_out_ref[b] = dot(picks, gate_ref[b])


def select_kernel(
    place_ref, *refs
):
    chunks = refs[:PLANES]
    slot_ref = refs[PLANES]
    row_refs = refs[PLANES + 1 : PLANES + 1 + GROUPS]
    hot_ref, high_ref, middle_ref, low_ref = refs[PLANES + 1 + GROUPS :]
    plane, group = place_ref[0], place_ref[1]
    q, r, o = slot_ref[0:1, :], slot_ref[1:2, :], slot_ref[2:3, :]
    expert = (plane * GROUPS + (q ^ group)).astype(F32)
    meta = jnp.concatenate([c[:, D:] for c in chunks], axis=0).astype(F32)
    named = jnp.zeros((COLUMN, ROWS), F32)
    parts = [jnp.zeros((COLUMN, ROWS), F32) for _ in range(3)]
    for k in range(TOPK):
        same = meta[:, k : k + 1] == expert
        named = jnp.where(same, 1.0, named)
        for i in range(3):
            at = (i + 1) * TOPK + k
            parts[i] = jnp.where(same, meta[:, at : at + 1], parts[i])
    row = lax.broadcasted_iota(jnp.int32, (COLUMN, COLUMN), 0)
    col = lax.broadcasted_iota(jnp.int32, (COLUMN, COLUMN), 1)
    earlier = jnp.where(((row >> 5) == (col >> 5)) & (col < row), 1.0, 0.0).astype(BF16)
    rank = dot(earlier, named.astype(BF16))
    token_plane = lax.broadcasted_iota(jnp.int32, (COLUMN, ROWS), 0) >> 5
    hit = (named > 0.5) & (rank == r.astype(F32)) & (token_plane == o)
    hot = jnp.where(hit, 1.0, 0.0)
    hot_ref[...] = hot.astype(BF16)
    for i, out_ref in enumerate((high_ref, middle_ref, low_ref)):
        out_ref[...] = jnp.where(hit, parts[i], 0.0).astype(BF16)
    across = hot.T.astype(BF16)
    for at in range(0, D, 512):
        tokens = jnp.concatenate([c[:, at : at + 512] for c in chunks], axis=0)
        picked = dot(across, tokens)
        for i, out_ref in enumerate(row_refs):
            out_ref[:, at : at + 512] = picked[i * SLOTS : (i + 1) * SLOTS].astype(BF16)


def expert_kernel(
    place_ref, g0, g1, g2, g3, up_ref, gate_ref, gate_mat, up_mat, down_mat, o0, o1, o2, o3
):
    own = place_ref[0] * GROUPS + place_ref[1]
    rows = jnp.concatenate([g[...].astype(F32) for g in (g0, g1, g2, g3)], axis=0).astype(BF16)
    back = dot(rows, down_mat[...], NT)
    gate = gate_ref[...]
    sigma = 1.0 / (1.0 + jnp.exp(-gate))
    activated = gate * sigma
    up = up_ref[...]
    d_up = back * activated
    weight = jnp.sum(d_up * up, axis=1, keepdims=True)
    d_gate = (back * up * sigma * (1.0 + gate * (1.0 - sigma))).astype(BF16)
    d_up = d_up.astype(BF16)
    lane = lax.broadcasted_iota(jnp.int32, (ROWS, EXTRA), 1)
    extra = jnp.where(lane == own, weight, 0.0)
    outs = (o0, o1, o2, o3)
    for i, out_ref in enumerate(outs):
        out_ref[:, D:] = extra[i * SLOTS : (i + 1) * SLOTS].astype(BF16)
    for at in range(0, D, 512):
        cut = slice(at, at + 512)
        grad = dot(d_gate, gate_mat[cut, :], NT) + dot(d_up, up_mat[cut, :], NT)
        for i, out_ref in enumerate(outs):
            out_ref[:, cut] = grad[i * SLOTS : (i + 1) * SLOTS].astype(BF16)


def combine_kernel(hot_ref, high_ref, middle_ref, low_ref, p0, p1, p2, p3, *outs):
    pairs = (p0, p1, p2, p3)
    for at in range(0, W, 512):
        cut = slice(at, min(at + 512, W))
        rows = jnp.concatenate([p[:, cut].astype(F32) for p in pairs], axis=0).astype(BF16)
        if at < D:
            mixed = dot(high_ref[...], rows) + dot(middle_ref[...], rows) + dot(low_ref[...], rows)
        else:
            mixed = dot(hot_ref[...], rows)
        for i, out_ref in enumerate(outs):
            out_ref[:, cut] = mixed[i * TOK : (i + 1) * TOK].astype(out_ref.dtype)


def token_kernel(own_ref, up_ref, down_ref, chunk_ref, x_ref, rms_ref, gain_ref, router_ref, out_ref):
    extra = slice(D, W)
    weights = own_ref[:, extra] + up_ref[:, extra].astype(F32) + down_ref[:, extra].astype(F32)
    meta = chunk_ref[:, extra].astype(F32)
    lane = lax.broadcasted_iota(jnp.int32, (TOK, EXTRA), 1).astype(F32)
    probs = jnp.zeros((TOK, EXTRA), F32)
    for k in range(TOPK):
        prob = (meta[:, TOPK + k : TOPK + k + 1] + meta[:, 2 * TOPK + k : 2 * TOPK + k + 1]) + meta[
            :, 3 * TOPK + k : 3 * TOPK + k + 1
        ]
        probs = jnp.where(meta[:, k : k + 1] == lane, prob, probs)
    centred = weights - jnp.sum(probs * weights, axis=1, keepdims=True)
    logit = probs * centred
    high, middle, low = split3(logit[:, : router_ref.shape[0]])
    router = router_ref[...]
    routed = dot(high, router) + dot(middle, router) + dot(low, router)
    mixed = own_ref[:, :D] + up_ref[:, :D].astype(F32) + down_ref[:, :D].astype(F32)
    gain = gain_ref[...].astype(F32)
    normed = x_ref[...].astype(F32) / gain
    scaled = gain * (mixed + routed)
    mean = jnp.sum(scaled * normed, axis=1, keepdims=True) * (1.0 / D)
    grad = chunk_ref[:, :D].astype(F32)
    out_ref[...] = (grad + rms_ref[...] * (scaled - normed * mean)).astype(BF16)


def body(
    out_grad,
    moe_input,
    expert_input,
    expert_gate,
    expert_ids,
    top_logits,
    inv_rms,
    norm_gain,
    w_gate,
    w_up,
    w_down,
    router,
):
    everyone = range(PLANES * GROUPS)
    index = lax.axis_index("expert")
    place = jnp.stack([index // GROUPS, index % GROUPS]).astype(jnp.int32)

    def along(array, by):
        pairs = [(i, (i + by * GROUPS) % (PLANES * GROUPS)) for i in everyone]
        return lax.ppermute(array, "expert", pairs)

    def swap(array, q):
        return lax.ppermute(array, "expert", [(i, i ^ q) for i in everyone])

    chunks = call(prep_kernel, (shape((TOK, W)), shape((TOK, W))), 3, smem_first=False)(
        out_grad[0], jnp.swapaxes(expert_ids[0], 1, 2), jnp.swapaxes(top_logits[0], 1, 2)
    )
    reach = ((4, 3), (3, 4))
    gathered = []
    for b in range(2):
        held = {0: chunks[b]}
        for step in range(1, 5):
            if step <= reach[b][0]:
                held[PLANES - step] = along(held[(PLANES - step + 1) % PLANES], 1)
            if step <= reach[b][1]:
                held[step] = along(held[step - 1], -1)
        gathered.append([held[o] for o in range(PLANES)])

    saved_x = jnp.transpose(expert_input[0, 0], (0, 2, 1, 3)).reshape(2, ROWS, D)
    saved_gate = jnp.transpose(expert_gate[0, 0], (0, 2, 1, 3)).reshape(2, ROWS, H)
    up_proj, gate_pre = call(
        saved_kernel,
        (shape((2, ROWS, H), F32), shape((2, ROWS, H), F32)),
        4,
        flops=2 * 2 * ROWS * D * (H + ROWS),
        nbytes=10_000_000,
    )(place, saved_x, saved_gate, SLOT_COL, w_up[0, 0])

    picked = []
    for b in range(2):
        outs = [shape((SLOTS, D))] * GROUPS + [shape((COLUMN, ROWS))] * 4
        result = call(
            select_kernel, outs, PLANES + 1, flops=2 * ROWS * COLUMN * D, nbytes=5_000_000
        )(place, *gathered[b], SLOT_ROW)
        rows = [result[0]] + [swap(result[q], q) for q in range(1, GROUPS)]
        picked.append((rows, result[GROUPS:]))

    returned = []
    for b in range(2):
        rows, _ = picked[b]
        grads = call(
            expert_kernel,
            [shape((SLOTS, W))] * GROUPS,
            9,
            flops=2 * 3 * ROWS * D * H,
            nbytes=14_000_000,
        )(place, *rows, up_proj[b], gate_pre[b], w_gate[0, 0], w_up[0, 0], w_down[0, 0])
        returned.append([grads[0]] + [swap(grads[q], q) for q in range(1, GROUPS)])

    sent = []
    for b in range(2):
        starts = (reach[b][0], PLANES - reach[b][1])
        outs = [shape((TOK, W), BF16 if o in starts else F32) for o in range(PLANES)]
        mixed = call(
            combine_kernel, outs, 8, flops=2 * 3 * ROWS * COLUMN * D, nbytes=5_000_000, smem_first=False
        )(*picked[b][1], *returned[b])
        upward, downward = mixed[starts[0]], mixed[starts[1]]
        for step in range(3, -1, -1):
            if step < reach[b][0]:
                upward = along(upward, 1)
                if step:
                    upward = (upward.astype(F32) + mixed[step]).astype(BF16)
            if step < reach[b][1]:
                downward = along(downward, -1)
                if step:
                    downward = (downward.astype(F32) + mixed[PLANES - step]).astype(BF16)
        layer_grad = call(token_kernel, shape((TOK, D)), 8, nbytes=1_500_000, smem_first=False)(
            mixed[0],
            upward,
            downward,
            chunks[b],
            moe_input[0, b],
            inv_rms[0, b][:, None],
            norm_gain,
            router[0].T,
        )
        length = lax.axis_size("pipe")
        by = 2 * b - 1
        pairs = [(i, i + by) for i in range(length) if 0 <= i + by < length]
        sent.append(lax.ppermute(layer_grad, "pipe", pairs))
    return jnp.stack(sent, axis=0)[None]


def solution(mesh):
    return jax.shard_map(
        body,
        mesh=mesh,
        in_specs=(
            P("pipe", None, "expert", None),
            P("pipe", None, "expert", None),
            P("pipe", "expert", None, None, None, None),
            P("pipe", "expert", None, None, None, None),
            P("pipe", None, "expert", None),
            P("pipe", None, "expert", None),
            P("pipe", None, "expert"),
            P("pipe", None),
            P("pipe", "expert", None, None),
            P("pipe", "expert", None, None),
            P("pipe", "expert", None, None),
            P("pipe", None, None),
        ),
        out_specs=P("pipe", None, "expert", None),
        check_vma=False,
    )
```

```python
import functools

import jax
import jax.numpy as jnp
import numpy as np
from jax import lax
from jax.experimental import pallas as pl
from jax.experimental.pallas import tpu as pltpu
from jax.sharding import PartitionSpec as P

PLANES = 8
GROUPS = 4
TOK = 32
TOPK = 8
CAP = 9
D = 2048
H = 768
EXTRA = 128
W = D + EXTRA
PARTS = ((0, 1, 7, 2, 6), (3, 5, 4))
PART_ROWS = (48, 32)
PART_AT = (0, 48)
BLOCK = sum(PART_ROWS)
ROWS = GROUPS * BLOCK
NT = (((1,), (1,)), ((), ()))
F32 = jnp.float32
BF16 = jnp.bfloat16
EMPTY = 100


def slot_block(planes, rows):
    rank = np.full(rows, EMPTY, np.int32)
    source = np.full(rows, EMPTY, np.int32)
    rank[: CAP * len(planes)] = np.repeat(np.arange(CAP), len(planes))
    source[: CAP * len(planes)] = np.tile(planes, CAP)
    return rank, source


def slot_rows(part):
    rank, source = slot_block(PARTS[part], PART_ROWS[part])
    group = np.repeat(np.arange(GROUPS), PART_ROWS[part])
    table = [group, np.tile(rank, GROUPS), np.tile(source, GROUPS)]
    return np.stack(table + table[:1] * 5).astype(np.int32)


def slot_columns():
    blocks = [slot_block(PARTS[i], PART_ROWS[i]) for i in range(2)]
    rank, source = (np.concatenate([block[i] for block in blocks]) for i in range(2))
    table = [np.repeat(np.arange(GROUPS), BLOCK), np.tile(rank, GROUPS), np.tile(source, GROUPS)]
    return np.ascontiguousarray(np.stack(table + table[:1] * 5).T.astype(np.int32))


SLOT_ROWS = (slot_rows(0), slot_rows(1))
SLOT_COLUMNS = slot_columns()

VMEM = pl.BlockSpec(memory_space=pltpu.VMEM)
SMEM = pl.BlockSpec(memory_space=pltpu.SMEM)
MIB = 1024 * 1024
LIMIT = 12 * MIB
ANY = pl.BlockSpec(memory_space=pl.ANY)


def call(kernel, outs, n_in, flops=0, nbytes=0, smem_first=True, after=0):
    specs = [VMEM] * n_in
    if smem_first:
        specs = [SMEM] + specs
    specs = specs + [ANY] * after
    return pl.pallas_call(
        kernel,
        out_shape=outs,
        in_specs=specs,
        out_specs=jax.tree.map(lambda _: VMEM, outs),
        compiler_params=pltpu.CompilerParams(vmem_limit_bytes=LIMIT),
        cost_estimate=pl.CostEstimate(flops=flops, bytes_accessed=nbytes, transcendentals=0),
    )


def pass_kernel(*_):
    pass


def held_until(arrays, needs):
    return pl.pallas_call(
        pass_kernel,
        out_shape=[jax.ShapeDtypeStruct(a.shape, a.dtype) for a in arrays],
        in_specs=[ANY] * (len(arrays) + len(needs)),
        out_specs=[ANY] * len(arrays),
        input_output_aliases={i: i for i in range(len(arrays))},
        compiler_params=pltpu.CompilerParams(vmem_limit_bytes=MIB),
    )(*arrays, *needs)


def shape(dims, dtype=BF16):
    return jax.ShapeDtypeStruct(dims, dtype)


def dot(a, b, dims=(((1,), (0,)), ((), ()))):
    return lax.dot_general(a, b, dims, preferred_element_type=F32)


def split3(value):
    high = value.astype(BF16)
    rest = value - high.astype(F32)
    middle = rest.astype(BF16)
    low = (rest - middle.astype(F32)).astype(BF16)
    return high, middle, low


def prep_kernel(grad_ref, ids_ref, logit_ref, first_ref, second_ref):
    row = lax.broadcasted_iota(jnp.int32, (TOK, TOK), 0)
    col = lax.broadcasted_iota(jnp.int32, (TOK, TOK), 1)
    eye = jnp.where(row == col, 1.0, 0.0).astype(BF16)
    for b, out_ref in enumerate((first_ref, second_ref)):
        logits = logit_ref[b]
        raised = jnp.exp(logits - jnp.max(logits, axis=0, keepdims=True))
        probs = raised / jnp.sum(raised, axis=0, keepdims=True)
        high, middle, low = split3(probs)
        stack = jnp.concatenate(
            [
                ids_ref[b].astype(F32),
                high.astype(F32),
                middle.astype(F32),
                low.astype(F32),
                jnp.zeros((EXTRA - 4 * TOPK, TOK), F32),
            ],
            axis=0,
        ).astype(BF16)
        out_ref[:, :D] = grad_ref[b]
        out_ref[:, D:] = dot(eye, stack, NT).astype(BF16)


def saved_kernel(b, place_ref, x_ref, gate_ref, slot_ref, up_mat_ref, *refs):
    up_ref, gate_out_ref = refs[-2:]
    plane, group = place_ref[0], place_ref[1]
    q, r, o = slot_ref[:, 0:1], slot_ref[:, 1:2], slot_ref[:, 2:3]
    wanted = r * (PLANES * GROUPS) + ((plane + o) & (PLANES - 1)) * GROUPS + (q ^ group)
    total = x_ref.shape[1]
    picks = jnp.where(
        wanted == lax.broadcasted_iota(jnp.int32, (ROWS, total), 1), 1.0, 0.0
    ).astype(BF16)
    rows = dot(picks, x_ref[b]).astype(BF16)
    up_ref[...] = dot(rows, up_mat_ref[...])
    gate_out_ref[...] = dot(picks, gate_ref[b])


def select_part(place_ref, part, chunks, slot_ref, row_refs, at_row, mask_refs):
    plane, group = place_ref[0], place_ref[1]
    q, r, o = slot_ref[0:1, :], slot_ref[1:2, :], slot_ref[2:3, :]
    count, slots = len(chunks) * TOK, slot_ref.shape[1]
    expert = (plane * GROUPS + (q ^ group)).astype(F32)
    meta = jnp.concatenate([c[:, D:] for c in chunks], axis=0).astype(F32)
    named = jnp.zeros((count, slots), F32)
    pieces = [jnp.zeros((count, slots), F32) for _ in range(3)]
    for k in range(TOPK):
        same = meta[:, k : k + 1] == expert
        named = jnp.where(same, 1.0, named)
        for i in range(3):
            at = (i + 1) * TOPK + k
            pieces[i] = jnp.where(same, meta[:, at : at + 1], pieces[i])
    row = lax.broadcasted_iota(jnp.int32, (count, count), 0)
    col = lax.broadcasted_iota(jnp.int32, (count, count), 1)
    earlier = jnp.where(((row >> 5) == (col >> 5)) & (col < row), 1.0, 0.0).astype(BF16)
    rank = dot(earlier, named.astype(BF16))
    block = lax.broadcasted_iota(jnp.int32, (count, slots), 0) >> 5
    token_plane = jnp.zeros((count, slots), jnp.int32)
    for i, at in enumerate(PARTS[part]):
        token_plane = jnp.where(block == i, at, token_plane)
    hit = (named > 0.5) & (rank == r.astype(F32)) & (token_plane == o)
    hot = jnp.where(hit, 1.0, 0.0)
    mask_refs[0][...] = hot.astype(BF16)
    for i in range(3):
        mask_refs[i + 1][...] = jnp.where(hit, pieces[i], 0.0).astype(BF16)
    across = hot.T.astype(BF16)
    size = PART_ROWS[part]
    for at in range(0, D, 512):
        tokens = jnp.concatenate([c[:, at : at + 512] for c in chunks], axis=0)
        picked = dot(across, tokens).astype(BF16)
        for i, out_ref in enumerate(row_refs):
            out_ref[at_row : at_row + size, at : at + 512] = picked[i * size : (i + 1) * size]


def select_kernel(parts, after, place_ref, *refs):
    refs = list(refs)
    chunks = [[refs.pop(0) for _ in PARTS[part]] for part in parts]
    slots = [refs.pop(0) for _ in parts]
    refs = refs[after:]
    row_refs = [refs.pop(0) for _ in range(GROUPS)]
    for i, part in enumerate(parts):
        at_row = PART_AT[part] if len(parts) > 1 else 0
        select_part(
            place_ref, part, chunks[i], slots[i], row_refs, at_row, refs[4 * i : 4 * i + 4]
        )


def expert_kernel(n_in, n_out, place_ref, *refs):
    refs = list(refs)
    given = [[refs.pop(0) for _ in range(GROUPS)] for _ in range(n_in)]
    up_ref, gate_ref, gate_mat, up_mat, down_mat = (refs.pop(0) for _ in range(5))
    outs = [[refs.pop(0) for _ in range(GROUPS)] for _ in range(n_out)]
    own = place_ref[0] * GROUPS + place_ref[1]
    rows = jnp.concatenate([part[q][...] for q in range(GROUPS) for part in given], axis=0)
    back = dot(rows, down_mat[...], NT)
    gate = gate_ref[...]
    sigma = 1.0 / (1.0 + jnp.exp(-gate))
    activated = gate * sigma
    up = up_ref[...]
    d_up = back * activated
    weight = jnp.sum(d_up * up, axis=1, keepdims=True)
    d_gate = (back * up * sigma * (1.0 + gate * (1.0 - sigma))).astype(BF16)
    d_up = d_up.astype(BF16)
    lane = lax.broadcasted_iota(jnp.int32, (ROWS, EXTRA), 1)
    extra = jnp.where(lane == own, weight, 0.0).astype(BF16)

    def put(columns, value):
        for q in range(GROUPS):
            at = q * BLOCK
            for part in outs:
                size = part[q].shape[0]
                part[q][:, columns] = value[at : at + size]
                at += size

    put(slice(D, W), extra)
    for at in range(0, D, 512):
        cut = slice(at, at + 512)
        grad = dot(d_gate, gate_mat[cut, :], NT) + dot(d_up, up_mat[cut, :], NT)
        put(cut, grad.astype(BF16))


def combine_kernel(parts, *refs):
    refs = list(refs)
    masks = [[refs.pop(0) for _ in range(4)] for _ in parts]
    pairs = [refs.pop(0) for _ in range(GROUPS)]
    for i, part in enumerate(parts):
        hot_ref, high_ref, middle_ref, low_ref = masks[i]
        outs = [refs.pop(0) for _ in PARTS[part]]
        at_row = PART_AT[part] if len(parts) > 1 else 0
        span = slice(at_row, at_row + PART_ROWS[part])
        for at in range(0, W, 512):
            cut = slice(at, min(at + 512, W))
            rows = jnp.concatenate([p[span, cut] for p in pairs], axis=0)
            if at < D:
                mixed = (
                    dot(high_ref[...], rows) + dot(middle_ref[...], rows) + dot(low_ref[...], rows)
                )
            else:
                mixed = dot(hot_ref[...], rows)
            for j, out_ref in enumerate(outs):
                out_ref[:, cut] = mixed[j * TOK : (j + 1) * TOK].astype(out_ref.dtype)


def token_kernel(own_ref, up_ref, down_ref, chunk_ref, x_ref, rms_ref, gain_ref, router_ref, out_ref):
    extra = slice(D, W)
    weights = own_ref[:, extra] + up_ref[:, extra].astype(F32) + down_ref[:, extra].astype(F32)
    meta = chunk_ref[:, extra].astype(F32)
    lane = lax.broadcasted_iota(jnp.int32, (TOK, EXTRA), 1).astype(F32)
    probs = jnp.zeros((TOK, EXTRA), F32)
    for k in range(TOPK):
        prob = (meta[:, TOPK + k : TOPK + k + 1] + meta[:, 2 * TOPK + k : 2 * TOPK + k + 1]) + meta[
            :, 3 * TOPK + k : 3 * TOPK + k + 1
        ]
        probs = jnp.where(meta[:, k : k + 1] == lane, prob, probs)
    centred = weights - jnp.sum(probs * weights, axis=1, keepdims=True)
    logit = probs * centred
    high, middle, low = split3(logit[:, : router_ref.shape[0]])
    router = router_ref[...]
    routed = dot(high, router) + dot(middle, router) + dot(low, router)
    mixed = own_ref[:, :D] + up_ref[:, :D].astype(F32) + down_ref[:, :D].astype(F32)
    gain = gain_ref[...].astype(F32)
    normed = x_ref[...].astype(F32) / gain
    scaled = gain * (mixed + routed)
    mean = jnp.sum(scaled * normed, axis=1, keepdims=True) * (1.0 / D)
    grad = chunk_ref[:, :D].astype(F32)
    out_ref[...] = (grad + rms_ref[...] * (scaled - normed * mean)).astype(BF16)


def body(
    out_grad,
    moe_input,
    expert_input,
    expert_gate,
    expert_ids,
    top_logits,
    inv_rms,
    norm_gain,
    w_gate,
    w_up,
    w_down,
    router,
):
    everyone = range(PLANES * GROUPS)
    index = lax.axis_index("expert")
    place = jnp.stack([index // GROUPS, index % GROUPS]).astype(jnp.int32)

    def along(array, by):
        pairs = [(i, (i + by * GROUPS) % (PLANES * GROUPS)) for i in everyone]
        return lax.ppermute(array, "expert", pairs)

    def swap(array, q):
        return lax.ppermute(array, "expert", [(i, i ^ q) for i in everyone])

    chunks = call(prep_kernel, (shape((TOK, W)), shape((TOK, W))), 3, smem_first=False)(
        out_grad[0], jnp.swapaxes(expert_ids[0], 1, 2), jnp.swapaxes(top_logits[0], 1, 2)
    )
    reach = ((4, 3), (3, 4))
    gathered = []
    for b in range(2):
        held = {0: chunks[b]}
        for step in range(1, 5):
            if step <= reach[b][0]:
                held[PLANES - step] = along(held[(PLANES - step + 1) % PLANES], 1)
            if step <= reach[b][1]:
                held[step] = along(held[step - 1], -1)
        gathered.append([held[o] for o in range(PLANES)])

    saved_x = jnp.transpose(expert_input[0, 0], (0, 2, 1, 3)).reshape(2, -1, D)
    saved_gate = jnp.transpose(expert_gate[0, 0], (0, 2, 1, 3)).reshape(2, -1, H)
    split_out, split_back = ((0,), (1,)), ((0, 1),)
    plans = ((split_out, split_back), (split_back, tuple(reversed(split_out))))

    def size(parts):
        return sum(PART_ROWS[part] for part in parts)

    def spread(arrays, needs=()):
        far = list(arrays[2:])
        if needs:
            far = held_until(far, needs)
        return [arrays[0], swap(arrays[1], 1), swap(far[0], 2), swap(far[1], 3)]

    def save(b, *after):
        return call(
            functools.partial(saved_kernel, b),
            (shape((ROWS, H), F32), shape((ROWS, H), F32)),
            4,
            flops=2 * ROWS * D * (H + ROWS),
            nbytes=5_000_000,
            after=len(after),
        )(place, saved_x, saved_gate, SLOT_COLUMNS, w_up[0, 0], *after)

    masks = [{}, {}]
    rows = [[], []]

    def select(b, parts, *after):
        outs = [shape((size(parts), D))] * GROUPS
        for part in parts:
            outs += [shape((len(PARTS[part]) * TOK, GROUPS * PART_ROWS[part]))] * 4
        chunk_refs = [gathered[b][o] for part in parts for o in PARTS[part]]
        slots = [SLOT_ROWS[part] for part in parts]
        result = call(
            functools.partial(select_kernel, parts, len(after)),
            outs,
            len(chunk_refs) + len(slots),
            flops=2 * ROWS * PLANES * TOK * D,
            nbytes=5_000_000,
            after=len(after),
        )(place, *chunk_refs, *slots, *after)
        for i, part in enumerate(parts):
            masks[b][part] = result[GROUPS + 4 * i : GROUPS + 4 * i + 4]
        return result[:GROUPS]

    near = spread(select(0, (0,)))
    far = spread(select(0, (1,), *near[2:]))
    whole = select(1, (0, 1), masks[0][1][3])
    held = held_until(whole[2:], far[2:])
    rows = [near + far, [whole[0], swap(whole[1], 1), swap(held[0], 2), swap(held[1], 3)]]
    saved = [save(0, held[0]), None]

    returned = []
    for b in range(2):
        wide = len(plans[b][1])
        outs = [shape((size(parts), W)) for parts in sorted(plans[b][1]) for _ in range(GROUPS)]
        grads = call(
            functools.partial(expert_kernel, len(plans[b][0]), wide),
            outs,
            len(rows[b]) + 5,
            flops=2 * 3 * ROWS * D * H,
            nbytes=14_000_000,
        )(place, *rows[b], *saved[b], w_gate[0, 0], w_up[0, 0], w_down[0, 0])
        if b == 0:
            saved[1] = save(1, grads[0])
        back = {}
        needs = ()
        for i, parts in reversed(list(enumerate(sorted(plans[b][1])))):
            back[parts] = spread(grads[GROUPS * i : GROUPS * (i + 1)], needs)
            needs = back[parts][2:]
        returned.append(back)

    sent = []
    for b in range(2):
        starts = (reach[b][0], PLANES - reach[b][1])
        mixed = {}
        for parts in plans[b][1]:
            places = [o for part in parts for o in PARTS[part]]
            outs = [shape((TOK, W), BF16 if o in starts else F32) for o in places]
            result = call(
                functools.partial(combine_kernel, parts),
                outs,
                4 * len(parts) + GROUPS,
                flops=2 * 3 * ROWS * PLANES * TOK * D,
                nbytes=5_000_000,
                smem_first=False,
            )(*[m for part in parts for m in masks[b][part]], *returned[b][parts])
            mixed.update(zip(places, result))
        upward, downward = mixed[starts[0]], mixed[starts[1]]
        for step in range(3, -1, -1):
            if step < reach[b][0]:
                upward = along(upward, 1)
                if step:
                    upward = (upward.astype(F32) + mixed[step]).astype(BF16)
            if step < reach[b][1]:
                downward = along(downward, -1)
                if step:
                    downward = (downward.astype(F32) + mixed[PLANES - step]).astype(BF16)
        layer_grad = call(token_kernel, shape((TOK, D)), 8, nbytes=1_500_000, smem_first=False)(
            mixed[0],
            upward,
            downward,
            chunks[b],
            moe_input[0, b],
            inv_rms[0, b][:, None],
            norm_gain,
            router[0].T,
        )
        length = lax.axis_size("pipe")
        by = 2 * b - 1
        pairs = [(i, i + by) for i in range(length) if 0 <= i + by < length]
        sent.append(lax.ppermute(layer_grad, "pipe", pairs))
    return jnp.stack(sent, axis=0)[None]


def solution(mesh):
    return jax.shard_map(
        body,
        mesh=mesh,
        in_specs=(
            P("pipe", None, "expert", None),
            P("pipe", None, "expert", None),
            P("pipe", "expert", None, None, None, None),
            P("pipe", "expert", None, None, None, None),
            P("pipe", None, "expert", None),
            P("pipe", None, "expert", None),
            P("pipe", None, "expert"),
            P("pipe", None),
            P("pipe", "expert", None, None),
            P("pipe", "expert", None, None),
            P("pipe", "expert", None, None),
            P("pipe", None, None),
        ),
        out_specs=P("pipe", None, "expert", None),
        check_vma=False,
    )
```

```python
import functools

import jax
import jax.numpy as jnp
import numpy as np
from jax import lax
from jax.experimental import pallas as pl
from jax.experimental.pallas import tpu as pltpu
from jax.sharding import PartitionSpec as P

PLANES = 8
GROUPS = 4
TOK = 32
TOPK = 8
CAP = 9
D = 2048
H = 768
EXTRA = 128
W = D + EXTRA
PARTS = ((0, 1, 7, 2, 6), (3, 5, 4))
PART_ROWS = (48, 32)
PART_AT = (0, 48)
BLOCK = sum(PART_ROWS)
ROWS = GROUPS * BLOCK
NT = (((1,), (1,)), ((), ()))
F32 = jnp.float32
BF16 = jnp.bfloat16
EMPTY = 100


def slot_block(planes, rows):
    rank = np.full(rows, EMPTY, np.int32)
    source = np.full(rows, EMPTY, np.int32)
    rank[: CAP * len(planes)] = np.repeat(np.arange(CAP), len(planes))
    source[: CAP * len(planes)] = np.tile(planes, CAP)
    return rank, source


def slot_rows(part):
    rank, source = slot_block(PARTS[part], PART_ROWS[part])
    group = np.repeat(np.arange(GROUPS), PART_ROWS[part])
    table = [group, np.tile(rank, GROUPS), np.tile(source, GROUPS)]
    return np.stack(table + table[:1] * 5).astype(np.int32)


def slot_columns():
    blocks = [slot_block(PARTS[i], PART_ROWS[i]) for i in range(2)]
    rank, source = (np.concatenate([block[i] for block in blocks]) for i in range(2))
    table = [np.repeat(np.arange(GROUPS), BLOCK), np.tile(rank, GROUPS), np.tile(source, GROUPS)]
    return np.ascontiguousarray(np.stack(table + table[:1] * 5).T.astype(np.int32))


SLOT_ROWS = (slot_rows(0), slot_rows(1))
SLOT_COLUMNS = slot_columns()

VMEM = pl.BlockSpec(memory_space=pltpu.VMEM)
SMEM = pl.BlockSpec(memory_space=pltpu.SMEM)
MIB = 1024 * 1024
LIMIT = 12 * MIB
ANY = pl.BlockSpec(memory_space=pl.ANY)


def call(kernel, outs, n_in, flops=0, nbytes=0, smem_first=True, after=0):
    specs = [VMEM] * n_in
    if smem_first:
        specs = [SMEM] + specs
    specs = specs + [ANY] * after
    return pl.pallas_call(
        kernel,
        out_shape=outs,
        in_specs=specs,
        out_specs=jax.tree.map(lambda _: VMEM, outs),
        compiler_params=pltpu.CompilerParams(vmem_limit_bytes=LIMIT),
        cost_estimate=pl.CostEstimate(flops=flops, bytes_accessed=nbytes, transcendentals=0),
    )


def pass_kernel(*_):
    pass


def held_until(arrays, needs):
    return pl.pallas_call(
        pass_kernel,
        out_shape=[jax.ShapeDtypeStruct(a.shape, a.dtype) for a in arrays],
        in_specs=[ANY] * (len(arrays) + len(needs)),
        out_specs=[ANY] * len(arrays),
        input_output_aliases={i: i for i in range(len(arrays))},
        compiler_params=pltpu.CompilerParams(vmem_limit_bytes=MIB),
    )(*arrays, *needs)


def shape(dims, dtype=BF16):
    return jax.ShapeDtypeStruct(dims, dtype)


def dot(a, b, dims=(((1,), (0,)), ((), ()))):
    return lax.dot_general(a, b, dims, preferred_element_type=F32)


def split3(value):
    high = value.astype(BF16)
    rest = value - high.astype(F32)
    middle = rest.astype(BF16)
    low = (rest - middle.astype(F32)).astype(BF16)
    return high, middle, low


def prep_kernel(grad_ref, ids_ref, logit_ref, first_ref, second_ref):
    row = lax.broadcasted_iota(jnp.int32, (TOK, TOK), 0)
    col = lax.broadcasted_iota(jnp.int32, (TOK, TOK), 1)
    eye = jnp.where(row == col, 1.0, 0.0).astype(BF16)
    for b, out_ref in enumerate((first_ref, second_ref)):
        logits = logit_ref[b]
        raised = jnp.exp(logits - jnp.max(logits, axis=0, keepdims=True))
        probs = raised / jnp.sum(raised, axis=0, keepdims=True)
        high, middle, low = split3(probs)
        stack = jnp.concatenate(
            [
                ids_ref[b].astype(F32),
                high.astype(F32),
                middle.astype(F32),
                low.astype(F32),
                jnp.zeros((EXTRA - 4 * TOPK, TOK), F32),
            ],
            axis=0,
        ).astype(BF16)
        out_ref[:, :D] = grad_ref[b]
        out_ref[:, D:] = dot(eye, stack, NT).astype(BF16)


def saved_kernel(b, place_ref, x_ref, gate_ref, slot_ref, up_mat_ref, *refs):
    up_ref, gate_out_ref = refs[-2:]
    plane, group = place_ref[0], place_ref[1]
    q, r, o = slot_ref[:, 0:1], slot_ref[:, 1:2], slot_ref[:, 2:3]
    wanted = r * (PLANES * GROUPS) + ((plane + o) & (PLANES - 1)) * GROUPS + (q ^ group)
    total = x_ref.shape[1]
    picks = jnp.where(
        wanted == lax.broadcasted_iota(jnp.int32, (ROWS, total), 1), 1.0, 0.0
    ).astype(BF16)
    rows = dot(picks, x_ref[b]).astype(BF16)
    up_ref[...] = dot(rows, up_mat_ref[...])
    gate_out_ref[...] = dot(picks, gate_ref[b])


def select_part(place_ref, part, chunks, slot_ref, row_refs, at_row, mask_refs):
    plane, group = place_ref[0], place_ref[1]
    q, r, o = slot_ref[0:1, :], slot_ref[1:2, :], slot_ref[2:3, :]
    count, slots = len(chunks) * TOK, slot_ref.shape[1]
    expert = (plane * GROUPS + (q ^ group)).astype(F32)
    meta = jnp.concatenate([c[:, D:] for c in chunks], axis=0).astype(F32)
    named = jnp.zeros((count, slots), F32)
    pieces = [jnp.zeros((count, slots), F32) for _ in range(3)]
    for k in range(TOPK):
        same = meta[:, k : k + 1] == expert
        named = jnp.where(same, 1.0, named)
        for i in range(3):
            at = (i + 1) * TOPK + k
            pieces[i] = jnp.where(same, meta[:, at : at + 1], pieces[i])
    row = lax.broadcasted_iota(jnp.int32, (count, count), 0)
    col = lax.broadcasted_iota(jnp.int32, (count, count), 1)
    earlier = jnp.where(((row >> 5) == (col >> 5)) & (col < row), 1.0, 0.0).astype(BF16)
    rank = dot(earlier, named.astype(BF16))
    block = lax.broadcasted_iota(jnp.int32, (count, slots), 0) >> 5
    token_plane = jnp.zeros((count, slots), jnp.int32)
    for i, at in enumerate(PARTS[part]):
        token_plane = jnp.where(block == i, at, token_plane)
    hit = (named > 0.5) & (rank == r.astype(F32)) & (token_plane == o)
    hot = jnp.where(hit, 1.0, 0.0)
    mask_refs[0][...] = hot.astype(BF16)
    for i in range(3):
        mask_refs[i + 1][...] = jnp.where(hit, pieces[i], 0.0).astype(BF16)
    across = hot.T.astype(BF16)
    size = PART_ROWS[part]
    for at in range(0, D, 512):
        tokens = jnp.concatenate([c[:, at : at + 512] for c in chunks], axis=0)
        picked = dot(across, tokens).astype(BF16)
        for i, out_ref in enumerate(row_refs):
            out_ref[at_row : at_row + size, at : at + 512] = picked[i * size : (i + 1) * size]


def select_kernel(parts, after, place_ref, *refs):
    refs = list(refs)
    chunks = [[refs.pop(0) for _ in PARTS[part]] for part in parts]
    slots = [refs.pop(0) for _ in parts]
    refs = refs[after:]
    row_refs = [refs.pop(0) for _ in range(GROUPS)]
    for i, part in enumerate(parts):
        at_row = PART_AT[part] if len(parts) > 1 else 0
        select_part(
            place_ref, part, chunks[i], slots[i], row_refs, at_row, refs[4 * i : 4 * i + 4]
        )


def expert_kernel(n_in, n_out, place_ref, *refs):
    refs = list(refs)
    given = [[refs.pop(0) for _ in range(GROUPS)] for _ in range(n_in)]
    up_ref, gate_ref, gate_mat, up_mat, down_mat = (refs.pop(0) for _ in range(5))
    outs = [[refs.pop(0) for _ in range(GROUPS)] for _ in range(n_out)]
    own = place_ref[0] * GROUPS + place_ref[1]
    rows = jnp.concatenate([part[q][...] for q in range(GROUPS) for part in given], axis=0)
    back = dot(rows, down_mat[...], NT)
    gate = gate_ref[...]
    sigma = 1.0 / (1.0 + jnp.exp(-gate))
    activated = gate * sigma
    up = up_ref[...]
    d_up = back * activated
    weight = jnp.sum(d_up * up, axis=1, keepdims=True)
    d_gate = (back * up * sigma * (1.0 + gate * (1.0 - sigma))).astype(BF16)
    d_up = d_up.astype(BF16)
    lane = lax.broadcasted_iota(jnp.int32, (ROWS, EXTRA), 1)
    extra = jnp.where(lane == own, weight, 0.0).astype(BF16)

    def put(columns, value):
        for q in range(GROUPS):
            at = q * BLOCK
            for part in outs:
                size = part[q].shape[0]
                part[q][:, columns] = value[at : at + size]
                at += size

    put(slice(D, W), extra)
    for at in range(0, D, 512):
        cut = slice(at, at + 512)
        grad = dot(d_gate, gate_mat[cut, :], NT) + dot(d_up, up_mat[cut, :], NT)
        put(cut, grad.astype(BF16))


def combine_kernel(parts, *refs):
    refs = list(refs)
    masks = [[refs.pop(0) for _ in range(4)] for _ in parts]
    pairs = [refs.pop(0) for _ in range(GROUPS)]
    for i, part in enumerate(parts):
        hot_ref, high_ref, middle_ref, low_ref = masks[i]
        outs = [refs.pop(0) for _ in PARTS[part]]
        at_row = PART_AT[part] if len(parts) > 1 else 0
        span = slice(at_row, at_row + PART_ROWS[part])
        for at in range(0, W, 512):
            cut = slice(at, min(at + 512, W))
            rows = jnp.concatenate([p[span, cut] for p in pairs], axis=0)
            if at < D:
                mixed = (
                    dot(high_ref[...], rows) + dot(middle_ref[...], rows) + dot(low_ref[...], rows)
                )
            else:
                mixed = dot(hot_ref[...], rows)
            for j, out_ref in enumerate(outs):
                out_ref[:, cut] = mixed[j * TOK : (j + 1) * TOK].astype(out_ref.dtype)


def add_kernel(count, after, *refs):
    for i in range(count):
        held_ref, term_ref, out_ref = refs[2 * i], refs[2 * i + 1], refs[2 * count + after + i]
        out_ref[...] = (held_ref[...].astype(F32) + term_ref[...]).astype(BF16)


def token_kernel(own_ref, up_ref, down_ref, chunk_ref, x_ref, rms_ref, gain_ref, router_ref, out_ref):
    extra = slice(D, W)
    weights = own_ref[:, extra] + up_ref[:, extra].astype(F32) + down_ref[:, extra].astype(F32)
    meta = chunk_ref[:, extra].astype(F32)
    lane = lax.broadcasted_iota(jnp.int32, (TOK, EXTRA), 1).astype(F32)
    probs = jnp.zeros((TOK, EXTRA), F32)
    for k in range(TOPK):
        prob = (meta[:, TOPK + k : TOPK + k + 1] + meta[:, 2 * TOPK + k : 2 * TOPK + k + 1]) + meta[
            :, 3 * TOPK + k : 3 * TOPK + k + 1
        ]
        probs = jnp.where(meta[:, k : k + 1] == lane, prob, probs)
    centred = weights - jnp.sum(probs * weights, axis=1, keepdims=True)
    logit = probs * centred
    high, middle, low = split3(logit[:, : router_ref.shape[0]])
    router = router_ref[...]
    routed = dot(high, router) + dot(middle, router) + dot(low, router)
    mixed = own_ref[:, :D] + up_ref[:, :D].astype(F32) + down_ref[:, :D].astype(F32)
    gain = gain_ref[...].astype(F32)
    normed = x_ref[...].astype(F32) / gain
    scaled = gain * (mixed + routed)
    mean = jnp.sum(scaled * normed, axis=1, keepdims=True) * (1.0 / D)
    grad = chunk_ref[:, :D].astype(F32)
    out_ref[...] = (grad + rms_ref[...] * (scaled - normed * mean)).astype(BF16)


def body(
    out_grad,
    moe_input,
    expert_input,
    expert_gate,
    expert_ids,
    top_logits,
    inv_rms,
    norm_gain,
    w_gate,
    w_up,
    w_down,
    router,
):
    everyone = range(PLANES * GROUPS)
    index = lax.axis_index("expert")
    place = jnp.stack([index // GROUPS, index % GROUPS]).astype(jnp.int32)

    def along(array, by):
        pairs = [(i, (i + by * GROUPS) % (PLANES * GROUPS)) for i in everyone]
        return lax.ppermute(array, "expert", pairs)

    def swap(array, q):
        return lax.ppermute(array, "expert", [(i, i ^ q) for i in everyone])

    chunks = call(prep_kernel, (shape((TOK, W)), shape((TOK, W))), 3, smem_first=False)(
        out_grad[0], jnp.swapaxes(expert_ids[0], 1, 2), jnp.swapaxes(top_logits[0], 1, 2)
    )
    reach = ((4, 3), (3, 4))
    gathered = []
    for b in range(2):
        held = {0: chunks[b]}
        for step in range(1, 5):
            if step <= reach[b][0]:
                held[PLANES - step] = along(held[(PLANES - step + 1) % PLANES], 1)
            if step <= reach[b][1]:
                held[step] = along(held[step - 1], -1)
        gathered.append([held[o] for o in range(PLANES)])

    saved_x = jnp.transpose(expert_input[0, 0], (0, 2, 1, 3)).reshape(2, -1, D)
    saved_gate = jnp.transpose(expert_gate[0, 0], (0, 2, 1, 3)).reshape(2, -1, H)
    split_out, split_back = ((0,), (1,)), ((0, 1),)
    plans = ((split_out, split_back), (split_out, tuple(reversed(split_out))))

    def size(parts):
        return sum(PART_ROWS[part] for part in parts)

    def spread(arrays, needs=()):
        far = list(arrays[2:])
        if needs:
            far = held_until(far, needs)
        return [arrays[0], swap(arrays[1], 1), swap(far[0], 2), swap(far[1], 3)]

    def save(b, *after):
        return call(
            functools.partial(saved_kernel, b),
            (shape((ROWS, H), F32), shape((ROWS, H), F32)),
            4,
            flops=2 * ROWS * D * (H + ROWS),
            nbytes=5_000_000,
            after=len(after),
        )(place, saved_x, saved_gate, SLOT_COLUMNS, w_up[0, 0], *after)

    masks = [{}, {}]
    rows = [[], []]

    def select(b, parts, *after):
        outs = [shape((size(parts), D))] * GROUPS
        for part in parts:
            outs += [shape((len(PARTS[part]) * TOK, GROUPS * PART_ROWS[part]))] * 4
        chunk_refs = [gathered[b][o] for part in parts for o in PARTS[part]]
        slots = [SLOT_ROWS[part] for part in parts]
        result = call(
            functools.partial(select_kernel, parts, len(after)),
            outs,
            len(chunk_refs) + len(slots),
            flops=2 * ROWS * PLANES * TOK * D,
            nbytes=5_000_000,
            after=len(after),
        )(place, *chunk_refs, *slots, *after)
        for i, part in enumerate(parts):
            masks[b][part] = result[GROUPS + 4 * i : GROUPS + 4 * i + 4]
        return result[:GROUPS]

    first_near = spread(select(0, (0,)))
    second_near = spread(select(1, (0,), masks[0][0][3]))
    saved = [save(0, masks[1][0][3]), None]
    first_far = spread(
        select(0, (1,), *first_near[2:], masks[1][0][3], saved[0][1]), second_near[2:3]
    )
    second_far = spread(select(1, (1,), masks[0][1][3]), first_far[2:3])
    rows = [first_near + first_far, second_near + second_far]

    mixed = [{}, {}]

    def combine(b, parts, pairs):
        starts = (reach[b][0], PLANES - reach[b][1])
        places = [o for part in parts for o in PARTS[part]]
        outs = [shape((TOK, W), BF16 if o in starts else F32) for o in places]
        result = call(
            functools.partial(combine_kernel, parts),
            outs,
            4 * len(parts) + GROUPS,
            flops=2 * 3 * ROWS * PLANES * TOK * D,
            nbytes=5_000_000,
            smem_first=False,
        )(*[m for part in parts for m in masks[b][part]], *pairs)
        mixed[b].update(zip(places, result))

    needs = (second_far[2],)
    for b in range(2):
        order = sorted(plans[b][1])
        outs = [shape((size(parts), W)) for parts in order for _ in range(GROUPS)]
        grads = call(
            functools.partial(expert_kernel, len(plans[b][0]), len(order)),
            outs,
            len(rows[b]) + 5,
            flops=2 * 3 * ROWS * D * H,
            nbytes=14_000_000,
        )(place, *rows[b], *saved[b], w_gate[0, 0], w_up[0, 0], w_down[0, 0])
        if b == 0:
            saved[1] = save(1, grads[0])
        for i, parts in reversed(list(enumerate(order))):
            pairs = spread(grads[GROUPS * i : GROUPS * (i + 1)], needs)
            needs = (pairs[2], mixed[0][0]) if b else (pairs[2],)
            combine(b, parts, pairs)

    held = [
        [mixed[b][reach[b][0]], mixed[b][PLANES - reach[b][1]]] for b in range(2)
    ]
    turn = ()
    for step in range(3, -1, -1):
        for b in range(2):
            moving = [i for i in range(2) if step < reach[b][i]]
            for i in moving:
                held[b][i] = along(held[b][i], 1 - 2 * i)
            if step:
                given = []
                for i in moving:
                    given += [held[b][i], mixed[b][step if i == 0 else PLANES - step]]
                result = call(
                    functools.partial(add_kernel, len(moving), len(turn)),
                    [shape((TOK, W))] * len(moving),
                    len(given),
                    nbytes=500_000,
                    smem_first=False,
                    after=len(turn),
                )(*given, *turn)
                for i, value in zip(moving, result):
                    held[b][i] = value
                turn = (result[0],)

    sent = []
    for b in range(2):
        layer_grad = call(token_kernel, shape((TOK, D)), 8, nbytes=1_500_000, smem_first=False)(
            mixed[b][0],
            held[b][0],
            held[b][1],
            chunks[b],
            moe_input[0, b],
            inv_rms[0, b][:, None],
            norm_gain,
            router[0].T,
        )
        length = lax.axis_size("pipe")
        by = 2 * b - 1
        pairs = [(i, i + by) for i in range(length) if 0 <= i + by < length]
        sent.append(lax.ppermute(layer_grad, "pipe", pairs))
    return jnp.stack(sent, axis=0)[None]


def solution(mesh):
    return jax.shard_map(
        body,
        mesh=mesh,
        in_specs=(
            P("pipe", None, "expert", None),
            P("pipe", None, "expert", None),
            P("pipe", "expert", None, None, None, None),
            P("pipe", "expert", None, None, None, None),
            P("pipe", None, "expert", None),
            P("pipe", None, "expert", None),
            P("pipe", None, "expert"),
            P("pipe", None),
            P("pipe", "expert", None, None),
            P("pipe", "expert", None, None),
            P("pipe", "expert", None, None),
            P("pipe", None, None),
        ),
        out_specs=P("pipe", None, "expert", None),
        check_vma=False,
    )
```

```python
import functools

import jax
import jax.numpy as jnp
from jax import lax
from jax.experimental import pallas as pl
from jax.experimental.pallas import tpu as pltpu
from jax.sharding import PartitionSpec as P

PLANES = 8
GROUPS = 4
TOK = 32
TOPK = 8
CAP = 9
D = 2048
H = 768
EXTRA = 128
W = D + EXTRA
PARTS = ((0, 1, 7, 2, 6), (3, 5, 4))
PART_ROWS = (48, 32)
PART_AT = (0, 48)
BLOCK = sum(PART_ROWS)
ROWS = GROUPS * BLOCK
NT = (((1,), (1,)), ((), ()))
F32 = jnp.float32
BF16 = jnp.bfloat16
EMPTY = 100


VMEM = pl.BlockSpec(memory_space=pltpu.VMEM)
SMEM = pl.BlockSpec(memory_space=pltpu.SMEM)
MIB = 1024 * 1024
LIMIT = 12 * MIB
ANY = pl.BlockSpec(memory_space=pl.ANY)


def slot_of(index, part):
    planes = PARTS[part]
    factor, shift = ((13, 6), (11, 5))[part]
    rank = (index * factor) >> shift
    nth = index - rank * len(planes)
    plane = jnp.zeros_like(index)
    for i, at in enumerate(planes):
        plane = jnp.where(nth == i, at, plane)
    return jnp.where(rank < CAP, rank, EMPTY), plane


def group_of(index, size):
    group = jnp.zeros_like(index)
    for i in range(1, GROUPS):
        group = jnp.where(index >= i * size, i, group)
    return group, index - group * size


def call(kernel, outs, n_in, flops=0, nbytes=0, smem_first=True, after=0):
    specs = [VMEM] * n_in
    if smem_first:
        specs = [SMEM] + specs
    specs = specs + [ANY] * after
    return pl.pallas_call(
        kernel,
        out_shape=outs,
        in_specs=specs,
        out_specs=jax.tree.map(lambda _: VMEM, outs),
        compiler_params=pltpu.CompilerParams(vmem_limit_bytes=LIMIT),
        cost_estimate=pl.CostEstimate(flops=flops, bytes_accessed=nbytes, transcendentals=0),
    )


def pass_kernel(*_):
    pass


def held_until(arrays, needs):
    return pl.pallas_call(
        pass_kernel,
        out_shape=[jax.ShapeDtypeStruct(a.shape, a.dtype) for a in arrays],
        in_specs=[ANY] * (len(arrays) + len(needs)),
        out_specs=[ANY] * len(arrays),
        input_output_aliases={i: i for i in range(len(arrays))},
        compiler_params=pltpu.CompilerParams(vmem_limit_bytes=MIB),
    )(*arrays, *needs)


def shape(dims, dtype=BF16):
    return jax.ShapeDtypeStruct(dims, dtype)


def dot(a, b, dims=(((1,), (0,)), ((), ()))):
    return lax.dot_general(a, b, dims, preferred_element_type=F32)


def split3(value):
    high = value.astype(BF16)
    rest = value - high.astype(F32)
    middle = rest.astype(BF16)
    low = (rest - middle.astype(F32)).astype(BF16)
    return high, middle, low


def prep_kernel(grad_ref, ids_ref, logit_ref, first_ref, second_ref):
    row = lax.broadcasted_iota(jnp.int32, (TOK, TOK), 0)
    col = lax.broadcasted_iota(jnp.int32, (TOK, TOK), 1)
    eye = jnp.where(row == col, 1.0, 0.0).astype(BF16)
    for b, out_ref in enumerate((first_ref, second_ref)):
        logits = logit_ref[b]
        raised = jnp.exp(logits - jnp.max(logits, axis=0, keepdims=True))
        probs = raised / jnp.sum(raised, axis=0, keepdims=True)
        high, middle, low = split3(probs)
        stack = jnp.concatenate(
            [
                ids_ref[b].astype(F32),
                high.astype(F32),
                middle.astype(F32),
                low.astype(F32),
                jnp.zeros((EXTRA - 4 * TOPK, TOK), F32),
            ],
            axis=0,
        ).astype(BF16)
        out_ref[:, :D] = grad_ref[b]
        out_ref[:, D:] = dot(eye, stack, NT).astype(BF16)


def saved_kernel(b, place_ref, x_ref, gate_ref, up_mat_ref, *refs):
    up_ref, gate_out_ref = refs[-2:]
    plane, group = place_ref[0], place_ref[1]
    q, within = group_of(lax.broadcasted_iota(jnp.int32, (ROWS, 1), 0), BLOCK)
    near, far = slot_of(within, 0), slot_of(within - PART_ROWS[0], 1)
    r, o = (jnp.where(within < PART_ROWS[0], near[i], far[i]) for i in range(2))
    wanted = r * (PLANES * GROUPS) + ((plane + o) & (PLANES - 1)) * GROUPS + (q ^ group)
    total = x_ref.shape[1]
    picks = jnp.where(
        wanted == lax.broadcasted_iota(jnp.int32, (ROWS, total), 1), 1.0, 0.0
    ).astype(BF16)
    rows = dot(picks, x_ref[b]).astype(BF16)
    up_ref[...] = dot(rows, up_mat_ref[...])
    gate_out_ref[...] = dot(picks, gate_ref[b])


def select_part(place_ref, part, chunks, row_refs, at_row, mask_refs):
    plane, group = place_ref[0], place_ref[1]
    count, slots = len(chunks) * TOK, GROUPS * PART_ROWS[part]
    q, within = group_of(lax.broadcasted_iota(jnp.int32, (1, slots), 1), PART_ROWS[part])
    r, o = slot_of(within, part)
    expert = (plane * GROUPS + (q ^ group)).astype(F32)
    meta = jnp.concatenate([c[:, D:] for c in chunks], axis=0).astype(F32)
    named = jnp.zeros((count, slots), F32)
    pieces = [jnp.zeros((count, slots), F32) for _ in range(3)]
    for k in range(TOPK):
        same = meta[:, k : k + 1] == expert
        named = jnp.where(same, 1.0, named)
        for i in range(3):
            at = (i + 1) * TOPK + k
            pieces[i] = jnp.where(same, meta[:, at : at + 1], pieces[i])
    row = lax.broadcasted_iota(jnp.int32, (count, count), 0)
    col = lax.broadcasted_iota(jnp.int32, (count, count), 1)
    earlier = jnp.where(((row >> 5) == (col >> 5)) & (col < row), 1.0, 0.0).astype(BF16)
    rank = dot(earlier, named.astype(BF16))
    block = lax.broadcasted_iota(jnp.int32, (count, slots), 0) >> 5
    token_plane = jnp.zeros((count, slots), jnp.int32)
    for i, at in enumerate(PARTS[part]):
        token_plane = jnp.where(block == i, at, token_plane)
    hit = (named > 0.5) & (rank == r.astype(F32)) & (token_plane == o)
    hot = jnp.where(hit, 1.0, 0.0)
    mask_refs[0][...] = hot.astype(BF16)
    for i in range(3):
        mask_refs[i + 1][...] = jnp.where(hit, pieces[i], 0.0).astype(BF16)
    across = hot.T.astype(BF16)
    size = PART_ROWS[part]
    for at in range(0, D, 512):
        tokens = jnp.concatenate([c[:, at : at + 512] for c in chunks], axis=0)
        picked = dot(across, tokens).astype(BF16)
        for i, out_ref in enumerate(row_refs):
            out_ref[at_row : at_row + size, at : at + 512] = picked[i * size : (i + 1) * size]


def select_kernel(parts, after, place_ref, *refs):
    refs = list(refs)
    chunks = [[refs.pop(0) for _ in PARTS[part]] for part in parts]
    refs = refs[after:]
    row_refs = [refs.pop(0) for _ in range(GROUPS)]
    for i, part in enumerate(parts):
        at_row = PART_AT[part] if len(parts) > 1 else 0
        select_part(
            place_ref, part, chunks[i], row_refs, at_row, refs[4 * i : 4 * i + 4]
        )


def expert_kernel(n_in, n_out, place_ref, *refs):
    refs = list(refs)
    given = [[refs.pop(0) for _ in range(GROUPS)] for _ in range(n_in)]
    up_ref, gate_ref, gate_mat, up_mat, down_mat = (refs.pop(0) for _ in range(5))
    outs = [[refs.pop(0) for _ in range(GROUPS)] for _ in range(n_out)]
    own = place_ref[0] * GROUPS + place_ref[1]
    rows = jnp.concatenate([part[q][...] for q in range(GROUPS) for part in given], axis=0)
    back = dot(rows, down_mat[...], NT)
    gate = gate_ref[...]
    sigma = 1.0 / (1.0 + jnp.exp(-gate))
    activated = gate * sigma
    up = up_ref[...]
    d_up = back * activated
    weight = jnp.sum(d_up * up, axis=1, keepdims=True)
    d_gate = (back * up * sigma * (1.0 + gate * (1.0 - sigma))).astype(BF16)
    d_up = d_up.astype(BF16)
    lane = lax.broadcasted_iota(jnp.int32, (ROWS, EXTRA), 1)
    extra = jnp.where(lane == own, weight, 0.0).astype(BF16)

    def put(columns, value):
        for q in range(GROUPS):
            at = q * BLOCK
            for part in outs:
                size = part[q].shape[0]
                part[q][:, columns] = value[at : at + size]
                at += size

    put(slice(D, W), extra)
    for at in range(0, D, 512):
        cut = slice(at, at + 512)
        grad = dot(d_gate, gate_mat[cut, :], NT) + dot(d_up, up_mat[cut, :], NT)
        put(cut, grad.astype(BF16))


def combine_kernel(parts, *refs):
    refs = list(refs)
    masks = [[refs.pop(0) for _ in range(4)] for _ in parts]
    pairs = [refs.pop(0) for _ in range(GROUPS)]
    for i, part in enumerate(parts):
        hot_ref, high_ref, middle_ref, low_ref = masks[i]
        outs = [refs.pop(0) for _ in PARTS[part]]
        at_row = PART_AT[part] if len(parts) > 1 else 0
        span = slice(at_row, at_row + PART_ROWS[part])
        for at in range(0, W, 512):
            cut = slice(at, min(at + 512, W))
            rows = jnp.concatenate([p[span, cut] for p in pairs], axis=0)
            if at < D:
                mixed = (
                    dot(high_ref[...], rows) + dot(middle_ref[...], rows) + dot(low_ref[...], rows)
                )
            else:
                mixed = dot(hot_ref[...], rows)
            for j, out_ref in enumerate(outs):
                out_ref[:, cut] = mixed[j * TOK : (j + 1) * TOK].astype(out_ref.dtype)


def add_kernel(count, after, *refs):
    for i in range(count):
        held_ref, term_ref, out_ref = refs[2 * i], refs[2 * i + 1], refs[2 * count + after + i]
        out_ref[...] = (held_ref[...].astype(F32) + term_ref[...]).astype(BF16)


def token_kernel(own_ref, up_ref, down_ref, chunk_ref, x_ref, rms_ref, gain_ref, router_ref, out_ref):
    extra = slice(D, W)
    weights = own_ref[:, extra] + up_ref[:, extra].astype(F32) + down_ref[:, extra].astype(F32)
    meta = chunk_ref[:, extra].astype(F32)
    lane = lax.broadcasted_iota(jnp.int32, (TOK, EXTRA), 1).astype(F32)
    probs = jnp.zeros((TOK, EXTRA), F32)
    for k in range(TOPK):
        prob = (meta[:, TOPK + k : TOPK + k + 1] + meta[:, 2 * TOPK + k : 2 * TOPK + k + 1]) + meta[
            :, 3 * TOPK + k : 3 * TOPK + k + 1
        ]
        probs = jnp.where(meta[:, k : k + 1] == lane, prob, probs)
    centred = weights - jnp.sum(probs * weights, axis=1, keepdims=True)
    logit = probs * centred
    high, middle, low = split3(logit[:, : router_ref.shape[0]])
    router = router_ref[...]
    routed = dot(high, router) + dot(middle, router) + dot(low, router)
    mixed = own_ref[:, :D] + up_ref[:, :D].astype(F32) + down_ref[:, :D].astype(F32)
    gain = gain_ref[...].astype(F32)
    normed = x_ref[...].astype(F32) / gain
    scaled = gain * (mixed + routed)
    mean = jnp.sum(scaled * normed, axis=1, keepdims=True) * (1.0 / D)
    grad = chunk_ref[:, :D].astype(F32)
    out_ref[...] = (grad + rms_ref[...] * (scaled - normed * mean)).astype(BF16)


def body(
    out_grad,
    moe_input,
    expert_input,
    expert_gate,
    expert_ids,
    top_logits,
    inv_rms,
    norm_gain,
    w_gate,
    w_up,
    w_down,
    router,
):
    everyone = range(PLANES * GROUPS)
    index = lax.axis_index("expert")
    place = jnp.stack([index // GROUPS, index % GROUPS]).astype(jnp.int32)

    def along(array, by):
        pairs = [(i, (i + by * GROUPS) % (PLANES * GROUPS)) for i in everyone]
        return lax.ppermute(array, "expert", pairs)

    def swap(array, q):
        return lax.ppermute(array, "expert", [(i, i ^ q) for i in everyone])

    chunks = call(prep_kernel, (shape((TOK, W)), shape((TOK, W))), 3, smem_first=False)(
        out_grad[0], jnp.swapaxes(expert_ids[0], 1, 2), jnp.swapaxes(top_logits[0], 1, 2)
    )
    reach = ((4, 3), (3, 4))
    gathered = []

    def gather(b, needs=()):
        held = {0: chunks[b]}
        for step in range(1, 5):
            if step == 3 and needs:
                held[PLANES - 2], held[2] = held_until([held[PLANES - 2], held[2]], needs)
            if step <= reach[b][0]:
                held[PLANES - step] = along(held[(PLANES - step + 1) % PLANES], 1)
            if step <= reach[b][1]:
                held[step] = along(held[step - 1], -1)
        gathered.append([held[o] for o in range(PLANES)])

    saved_x = jnp.transpose(expert_input[0, 0], (0, 2, 1, 3)).reshape(2, -1, D)
    saved_gate = jnp.transpose(expert_gate[0, 0], (0, 2, 1, 3)).reshape(2, -1, H)
    split_out, split_back = ((0,), (1,)), ((0, 1),)
    plans = ((split_out, split_back), (split_out, tuple(reversed(split_out))))

    def size(parts):
        return sum(PART_ROWS[part] for part in parts)

    def spread(arrays, needs=()):
        far = list(arrays[2:])
        if needs:
            far = held_until(far, needs)
        return [arrays[0], swap(arrays[1], 1), swap(far[0], 2), swap(far[1], 3)]

    def save(b, *after):
        return call(
            functools.partial(saved_kernel, b),
            (shape((ROWS, H), F32), shape((ROWS, H), F32)),
            3,
            flops=2 * ROWS * D * (H + ROWS),
            nbytes=5_000_000,
            after=len(after),
        )(place, saved_x, saved_gate, w_up[0, 0], *after)

    masks = [{}, {}]
    rows = [[], []]

    def select(b, parts, *after):
        outs = [shape((size(parts), D))] * GROUPS
        for part in parts:
            outs += [shape((len(PARTS[part]) * TOK, GROUPS * PART_ROWS[part]))] * 4
        chunk_refs = [gathered[b][o] for part in parts for o in PARTS[part]]
        result = call(
            functools.partial(select_kernel, parts, len(after)),
            outs,
            len(chunk_refs),
            flops=2 * ROWS * PLANES * TOK * D,
            nbytes=5_000_000,
            after=len(after),
        )(place, *chunk_refs, *after)
        for i, part in enumerate(parts):
            masks[b][part] = result[GROUPS + 4 * i : GROUPS + 4 * i + 4]
        return result[:GROUPS]

    gather(0)
    first_near = spread(select(0, (0,)))
    gather(1, (masks[0][0][3],))
    second_near = spread(select(1, (0,), masks[0][0][3]))
    first_far = spread(select(0, (1,), *first_near[2:], masks[1][0][3]), second_near[2:3])
    saved = [save(0, masks[0][1][3]), None]
    second_far = spread(select(1, (1,), saved[0][1]), first_far[2:3])
    rows = [first_near + first_far, second_near + second_far]

    mixed = [{}, {}]

    def combine(b, parts, pairs):
        starts = (reach[b][0], PLANES - reach[b][1])
        places = [o for part in parts for o in PARTS[part]]
        outs = [shape((TOK, W), BF16 if o in starts else F32) for o in places]
        result = call(
            functools.partial(combine_kernel, parts),
            outs,
            4 * len(parts) + GROUPS,
            flops=2 * 3 * ROWS * PLANES * TOK * D,
            nbytes=5_000_000,
            smem_first=False,
        )(*[m for part in parts for m in masks[b][part]], *pairs)
        mixed[b].update(zip(places, result))

    needs = (second_far[2],)
    for b in range(2):
        order = sorted(plans[b][1])
        outs = [shape((size(parts), W)) for parts in order for _ in range(GROUPS)]
        grads = call(
            functools.partial(expert_kernel, len(plans[b][0]), len(order)),
            outs,
            len(rows[b]) + 5,
            flops=2 * 3 * ROWS * D * H,
            nbytes=14_000_000,
        )(place, *rows[b], *saved[b], w_gate[0, 0], w_up[0, 0], w_down[0, 0])
        if b == 0:
            saved[1] = save(1, grads[0])
        for i, parts in reversed(list(enumerate(order))):
            pairs = spread(grads[GROUPS * i : GROUPS * (i + 1)], needs)
            needs = (pairs[2], mixed[0][0]) if b else (pairs[2],)
            combine(b, parts, pairs)

    held = [
        [mixed[b][reach[b][0]], mixed[b][PLANES - reach[b][1]]] for b in range(2)
    ]
    turn = ()
    for step in range(3, -1, -1):
        for b in range(2):
            moving = [i for i in range(2) if step < reach[b][i]]
            for i in moving:
                held[b][i] = along(held[b][i], 1 - 2 * i)
            if step:
                given = []
                for i in moving:
                    given += [held[b][i], mixed[b][step if i == 0 else PLANES - step]]
                result = call(
                    functools.partial(add_kernel, len(moving), len(turn)),
                    [shape((TOK, W))] * len(moving),
                    len(given),
                    nbytes=500_000,
                    smem_first=False,
                    after=len(turn),
                )(*given, *turn)
                for i, value in zip(moving, result):
                    held[b][i] = value
                turn = (result[0],)

    sent = []
    for b in range(2):
        layer_grad = call(token_kernel, shape((TOK, D)), 8, nbytes=1_500_000, smem_first=False)(
            mixed[b][0],
            held[b][0],
            held[b][1],
            chunks[b],
            moe_input[0, b],
            inv_rms[0, b][:, None],
            norm_gain,
            router[0].T,
        )
        length = lax.axis_size("pipe")
        by = 2 * b - 1
        pairs = [(i, i + by) for i in range(length) if 0 <= i + by < length]
        sent.append(lax.ppermute(layer_grad, "pipe", pairs))
    return jnp.stack(sent, axis=0)[None]


def solution(mesh):
    return jax.shard_map(
        body,
        mesh=mesh,
        in_specs=(
            P("pipe", None, "expert", None),
            P("pipe", None, "expert", None),
            P("pipe", "expert", None, None, None, None),
            P("pipe", "expert", None, None, None, None),
            P("pipe", None, "expert", None),
            P("pipe", None, "expert", None),
            P("pipe", None, "expert"),
            P("pipe", None),
            P("pipe", "expert", None, None),
            P("pipe", "expert", None, None),
            P("pipe", "expert", None, None),
            P("pipe", None, None),
        ),
        out_specs=P("pipe", None, "expert", None),
        check_vma=False,
    )
```
